512 devices in a mesh: rows: 8 (over x, core), cols: 8 (over z_lo), depth: 8 (over z_hi, y).
Axes of the slice: x: 4, y: 4, z: 16 (z_hi: 2, z_lo: 8; z = z_hi * 8 + z_lo), core: 2. Of those that a mesh axis runs over, the one named last changes fastest.
Arguments:
- activations: bfloat16 [512, 8192], P(('cols', 'depth'), 'rows'), may hold values from -6 to 6
- out_grad: bfloat16 [512, 8192], P(('cols', 'depth'), 'rows'), may hold values from -1.5 to 1.5
- w_gate: bfloat16 [8192, 16384], P('rows', ('cols', 'depth')), may hold values from -0.0625 to 0.0625
- w_up: bfloat16 [8192, 16384], P('rows', ('cols', 'depth')), may hold values from -0.0625 to 0.0625
- w_down: bfloat16 [16384, 8192], P(('cols', 'depth'), 'rows'), may hold values from -0.046875 to 0.046875
Outputs:
- input_grad: bfloat16 [512, 8192], P(('cols', 'depth'), 'rows')
- gate_grad: bfloat16 [8192, 16384], P('rows', ('cols', 'depth'))
- up_grad: bfloat16 [8192, 16384], P('rows', ('cols', 'depth'))
- down_grad: bfloat16 [16384, 8192], P(('cols', 'depth'), 'rows')
The draws below stay inside these ranges and needn't reach their ends.
All inputs are finite; a program needn't handle non-finite values.
Results may differ from the reference program's by a relative error of at most 0.0049.
Values may be sent and summed in bfloat16 or wider, within the bound.
A program may use at most 64 MiB of HBM per device.

```python
import jax
import jax.numpy as jnp

D = 8192
FF = 16384
TOKENS = 512


def block_levels(own_key, dims, split, low, largest):
    def one(position, shards_of):
        heights = jax.random.uniform(jax.random.fold_in(jax.random.fold_in(own_key, 6), position), (shards_of,), jnp.float32, low / len(split), largest / len(split))
        return jnp.repeat(jnp.exp(heights), dims[position] // shards_of).reshape((-1,) + (1,) * (len(dims) - position - 1))

    loudness = one(*split[0])
    for cut in split[1:]:
        loudness = loudness * one(*cut)
    return loudness


def gaussian(key, extent, spread, limit, pieces=(), kind=jnp.bfloat16):
    values = jax.random.normal(key, extent, jnp.float32) * spread
    if len(pieces) > 0:
        values = block_levels(key, extent, pieces, -0.22, 0.18) * values
    return jnp.clip(values, min=-limit, max=limit).astype(kind)


def setup_inputs(seed: int = 0) -> dict:
    key_of = jax.random.split(jax.random.key(seed), 6)
    return {
        "activations": gaussian(key_of[0], (TOKENS, D), 1.0, 6.0, ((0, 64), (1, 8))),
        "out_grad": gaussian(key_of[1], (TOKENS, D), 0.25, 1.5, ((0, 64), (1, 8))),
        "w_gate": gaussian(key_of[2], (D, FF), D ** -0.5, 0.0625, ((0, 8), (1, 64))),
        "w_up": gaussian(key_of[3], (D, FF), D ** -0.5, 0.0625, ((0, 8), (1, 64))),
        "w_down": gaussian(key_of[4], (FF, D), FF ** -0.5, 0.046875, ((0, 64), (1, 8))),
    }


def reference(activations, out_grad, w_gate, w_up, w_down):
    gate = jnp.dot(activations, w_gate, preferred_element_type=jnp.float32)
    up = jnp.dot(activations, w_up, preferred_element_type=jnp.float32)
    hid_grad = jnp.einsum('td,fd->tf', out_grad, w_down, preferred_element_type=jnp.float32)
    sigm = jax.nn.sigmoid(gate)
    hidden = (gate * sigm * up).astype(jnp.bfloat16)
    gate_delta = (hid_grad * up * sigm * (1.0 + gate * (1.0 - sigm))).astype(jnp.bfloat16)
    up_delta = (hid_grad * gate * sigm).astype(jnp.bfloat16)
    down_grad = jnp.einsum('tf,td->fd', hidden, out_grad, preferred_element_type=jnp.float32).astype(jnp.bfloat16)
    gate_grad = jnp.einsum('td,tf->df', activations, gate_delta, preferred_element_type=jnp.float32).astype(jnp.bfloat16)
    up_grad = jnp.einsum('td,tf->df', activations, up_delta, preferred_element_type=jnp.float32).astype(jnp.bfloat16)
    input_total = jnp.einsum('tf,df->td', gate_delta, w_gate, preferred_element_type=jnp.float32)
    input_total = input_total + jnp.einsum('tf,df->td', up_delta, w_up, preferred_element_type=jnp.float32)
    return input_total.astype(jnp.bfloat16), gate_grad, up_grad, down_grad
```

```python
import jax
import jax.numpy as jnp
from jax import lax
from jax.experimental import pallas as pl
from jax.experimental.pallas import tpu as pltpu
from jax.sharding import PartitionSpec as P

BF = jnp.bfloat16
F32 = jnp.float32
NR, NY, NZ, ZLO = 8, 4, 16, 8
CHUNKS = 4
NT = (((1,), (1,)), ((), ()))
TN = (((0,), (0,)), ((), ()))


def dot(a, b, dims=(((1,), (0,)), ((), ()))):
    return lax.dot_general(a, b, dims, preferred_element_type=F32)


def kernel(
    act_ref, grad_ref, wg_hbm, wu_hbm, wd_hbm,
    ig_ref, gg_hbm, ug_hbm, dg_hbm,
    xa, xb, acts, grads, wg, wu, wd, part, own_part, bsend, brecv, delta,
    total, own_total, ysend, yrecv, own_z, zsend, zrecv, gg, ug, dg,
    w_sem, o_sem, xa_recv, xb_recv, y0_recv, y_recv, b_recv, c_recv, dy_recv, dz_recv,
    xa_send, xb_send, y0_send, y_send, b_send, c_send, dy_send, dz_send,
):
    r = lax.axis_index("rows")
    zl = lax.axis_index("cols")
    dp = lax.axis_index("depth")
    y = lax.rem(dp, NY)
    z = lax.div(dp, NY) * ZLO + zl

    def row_peer(k):
        return {"rows": lax.rem(r + k, NR), "cols": zl, "depth": dp}

    def y_peer(k):
        return {"rows": r, "cols": zl, "depth": dp - y + lax.rem(y + k, NY)}

    def z_peer(k):
        t = lax.rem(z + (k + NZ), NZ)
        return {"rows": r, "cols": lax.rem(t, ZLO), "depth": lax.div(t, ZLO) * NY + y}

    def send(src, dst, ssem, rsem, dev):
        pltpu.make_async_remote_copy(
            src_ref=src, dst_ref=dst, send_sem=ssem, recv_sem=rsem,
            device_id=dev, device_id_type=pl.DeviceIdType.MESH,
        ).start()

    def drain(ref, sem):
        pltpu.make_async_copy(ref, ref, sem).wait()

    w_copies = [
        pltpu.make_async_copy(src, dst, w_sem.at[i])
        for i, (src, dst) in enumerate(((wg_hbm, wg), (wu_hbm, wu), (wd_hbm, wd)))
    ]
    for c in w_copies:
        c.start()

    mine = jnp.concatenate([act_ref[...].astype(F32), grad_ref[...].astype(F32)], axis=0).astype(BF)
    xa[0, y] = mine[:, :512]
    xb[0, y] = mine[:, 512:]

    barrier = pltpu.get_barrier_semaphore()
    peers = [row_peer(k) for k in range(1, NR)]
    peers += [y_peer(k) for k in range(1, NY)]
    peers += [z_peer(k) for k in range(1, NZ)]
    for p in peers:
        pl.semaphore_signal(barrier, inc=1, device_id=p, device_id_type=pl.DeviceIdType.MESH)
    pl.semaphore_wait(barrier, len(peers))

    def start_gather():
        for k in range(1, NY):
            send(xa.at[0, y], xa.at[0, y], y0_send, y0_recv, y_peer(k))
        send(xb.at[0, y], xb.at[1, y], xb_send.at[0], xb_recv.at[1], z_peer(1))
        send(xb.at[0, y], xb.at[2, y], xb_send.at[16], xb_recv.at[2], z_peer(-1))
        for k in range(1, NY):
            send(xb.at[0, y], xb.at[0, y], y_send.at[0], y_recv.at[0], y_peer(k))
        drain(xa.at[0, pl.ds(0, 3)], y0_recv)
        send(xa.at[0], xa.at[1], xa_send.at[0], xa_recv.at[1], z_peer(1))
        send(xa.at[0], xa.at[2], xa_send.at[16], xa_recv.at[2], z_peer(-1))

    def y_forward(slot):
        for k in range(1, NY):
            send(xb.at[slot, y], xb.at[slot, y], y_send.at[slot], y_recv.at[slot], y_peer(k))

    def gather_step(d):
        if d == 8:
            drain(xb.at[15, y], xb_recv.at[15])
            y_forward(15)
            drain(xa.at[15, pl.ds(0, 2)], xa_recv.at[15])
            drain(xa.at[15, pl.ds(2, 2)], xa_recv.at[16])
            return
        for slot, to in ((2 * d - 1, 1), (2 * d, -1)):
            drain(xb.at[slot, y], xb_recv.at[slot])
            if d < 7:
                send(xb.at[slot, y], xb.at[slot + 2, y], xb_send.at[slot], xb_recv.at[slot + 2], z_peer(to))
            elif to == -1:
                send(xb.at[slot, y], xb.at[15, y], xb_send.at[slot], xb_recv.at[15], z_peer(to))
            drain(xa.at[slot], xa_recv.at[slot])
            if d < 7:
                send(xa.at[slot], xa.at[slot + 2], xa_send.at[slot], xa_recv.at[slot + 2], z_peer(to))
            else:
                half = pl.ds(0, 2) if to == 1 else pl.ds(2, 2)
                send(xa.at[slot, half], xa.at[15, half], xa_send.at[slot],
                     xa_recv.at[15 if to == 1 else 16], z_peer(to))
            y_forward(slot)

    def partial_sums(c):
        for s in range(4 * c, 4 * c + 4):
            drain(xb.at[s, pl.ds(0, 3)], y_recv.at[s])

        def pick(p, carry):
            s = 4 * c + lax.div(p, 2)
            y0 = lax.rem(p, 2) * 2
            rows = pl.ds(pl.multiple_of(c * 128 + p * 16, 16), 16)
            for buf, cols in ((xa, pl.ds(0, 512)), (xb, pl.ds(512, 512))):
                b0 = buf[s, y0].astype(F32)
                b1 = buf[s, y0 + 1].astype(F32)
                acts[rows, cols] = jnp.concatenate([b0[:8], b1[:8]], axis=0).astype(BF)
                grads[rows, cols] = jnp.concatenate([b0[8:], b1[8:]], axis=0).astype(BF)
            return carry

        lax.fori_loop(0, 8, pick, 0)
        rows = pl.ds(c * 128, 128)
        part[:, 0:256] = dot(acts[rows], wg[...])
        part[:, 256:512] = dot(acts[rows], wu[...])
        part[:, 512:768] = dot(grads[rows], wd[...], NT)
        bsend[c] = part[...].astype(BF).reshape(NR, 16, 768)
        own_part[c] = part[pl.ds(pl.multiple_of(r * 16, 16), 16)]
        for k in range(1, NR):
            send(bsend.at[c, lax.rem(r + k, NR)], brecv.at[c, k - 1], b_send.at[c], b_recv.at[c], row_peer(k))

    def pointwise(c):
        drain(brecv.at[c], b_recv.at[c])
        tot = own_part[c]
        for k in range(NR - 1):
            tot = tot + brecv[c, k].astype(F32)
        gate, up, hid = tot[:, 0:256], tot[:, 256:512], tot[:, 512:768]
        sig = 1.0 / (1.0 + jnp.exp(-gate))
        delta[c, r, :, 0:256] = (gate * sig * up).astype(BF)
        delta[c, r, :, 256:512] = (hid * up * sig * (1.0 + gate * (1.0 - sig))).astype(BF)
        delta[c, r, :, 512:768] = (hid * gate * sig).astype(BF)
        for k in range(1, NR):
            send(delta.at[c, r], delta.at[c, r], c_send.at[c], c_recv.at[c], row_peer(k))

    def input_terms(c):
        drain(delta.at[c, pl.ds(0, NR - 1)], c_recv.at[c])
        dl = delta[c].reshape(128, 768)
        total[...] = (dot(dl[:, 256:512], wg[...], NT) + dot(dl[:, 512:768], wu[...], NT)).reshape(4, NY, 8, 1024)
        for t in range(NY):
            ysend[c, t] = jnp.concatenate([total[s, t] for s in range(4)], axis=0).astype(BF)
        for s in range(4):
            own_total[c, s] = total[s, y]
        for k in range(1, NY):
            send(ysend.at[c, lax.rem(y + k, NY)], yrecv.at[c, k - 1], dy_send.at[c], dy_recv.at[c], y_peer(k))

    def slot_offset(slot):
        return -((slot + 1) // 2) if slot % 2 else slot // 2

    def reduce_y(c):
        drain(yrecv.at[c], dy_recv.at[c])
        for s in range(4):
            slot = 4 * c + s
            if s % 2 == 0:
                got = [yrecv[c, k, 8 * s:8 * s + 16, :].astype(F32) for k in range(NY - 1)]
            lo = 8 * (s % 2)
            v = own_total[c, s] + (got[0][lo:lo + 8] + got[1][lo:lo + 8] + got[2][lo:lo + 8])
            v = jnp.concatenate([v[:, :512], v[:, 512:]], axis=0)
            if slot == 0:
                own_z[...] = v
            else:
                zsend[slot - 1] = v.astype(BF)
        for s in range(4):
            slot = 4 * c + s
            if slot:
                k = slot_offset(slot) % NZ
                send(zsend.at[slot - 1], zrecv.at[k - 1], dz_send, dz_recv, z_peer(k))

    def reduce_z():
        drain(zrecv, dz_recv)
        v = own_z[...]
        for k in range(NZ - 1):
            v = v + zrecv[k].astype(F32)
        ig_ref[...] = jnp.concatenate([v[:8], v[8:]], axis=1).astype(BF)

    def weight_grads():
        dl = delta[...].reshape(512, 768)
        gg[...] = dot(acts[...], dl[:, 256:512], TN).astype(BF)
        ug[...] = dot(acts[...], dl[:, 512:768], TN).astype(BF)
        dg[...] = dot(dl[:, 0:256], grads[...], TN).astype(BF)

    out_copies = [
        pltpu.make_async_copy(src, dst, o_sem.at[i])
        for i, (src, dst) in enumerate(((gg, gg_hbm), (ug, ug_hbm), (dg, dg_hbm)))
    ]

    start_gather()
    gather_step(1)
    for c in w_copies:
        c.wait()
    gather_step(2)
    partial_sums(0)
    gather_step(3)
    pointwise(0)
    gather_step(4)
    partial_sums(1)
    input_terms(0)
    gather_step(5)
    pointwise(1)
    reduce_y(0)
    gather_step(6)
    partial_sums(2)
    input_terms(1)
    gather_step(7)
    pointwise(2)
    reduce_y(1)
    gather_step(8)
    partial_sums(3)
    input_terms(2)
    pointwise(3)
    reduce_y(2)
    input_terms(3)
    weight_grads()
    for c in out_copies:
        c.start()
    reduce_y(3)
    reduce_z()

    drain(xa.at[0, pl.ds(0, 3)], y0_send)
    for s in (0, 16, *range(1, 13)):
        drain(xa.at[min(s, 15)], xa_send.at[s])
    for s in (13, 14):
        drain(xa.at[s, pl.ds(0, 2)], xa_send.at[s])
    for s in (0, 16, *range(1, 13), 14):
        drain(xb.at[min(s, 15), 0], xb_send.at[s])
    for s in range(16):
        drain(xb.at[s, pl.ds(0, 3)], y_send.at[s])
    for c in range(CHUNKS):
        drain(brecv.at[c], b_send.at[c])
        drain(delta.at[c, pl.ds(0, NR - 1)], c_send.at[c])
        drain(yrecv.at[c], dy_send.at[c])
    drain(zsend, dz_send)
    for c in out_copies:
        c.wait()


def body(activations, out_grad, w_gate, w_up, w_down):
    vmem = pl.BlockSpec(memory_space=pltpu.VMEM)
    hbm = pl.BlockSpec(memory_space=pl.ANY)
    dma = pltpu.SemaphoreType.DMA
    return pl.pallas_call(
        kernel,
        out_shape=(
            jax.ShapeDtypeStruct((8, 1024), BF),
            jax.ShapeDtypeStruct((1024, 256), BF),
            jax.ShapeDtypeStruct((1024, 256), BF),
            jax.ShapeDtypeStruct((256, 1024), BF),
        ),
        in_specs=[vmem, vmem, hbm, hbm, hbm],
        out_specs=(vmem, hbm, hbm, hbm),
        scratch_shapes=[
            pltpu.VMEM((16, 4, 16, 512), BF),
            pltpu.VMEM((16, 4, 16, 512), BF),
            pltpu.VMEM((512, 1024), BF),
            pltpu.VMEM((512, 1024), BF),
            pltpu.VMEM((1024, 256), BF),
            pltpu.VMEM((1024, 256), BF),
            pltpu.VMEM((256, 1024), BF),
            pltpu.VMEM((128, 768), F32),
            pltpu.VMEM((CHUNKS, 16, 768), F32),
            pltpu.VMEM((CHUNKS, NR, 16, 768), BF),
            pltpu.VMEM((CHUNKS, NR - 1, 16, 768), BF),
            pltpu.VMEM((CHUNKS, NR, 16, 768), BF),
            pltpu.VMEM((4, NY, 8, 1024), F32),
            pltpu.VMEM((CHUNKS, 4, 8, 1024), F32),
            pltpu.VMEM((CHUNKS, NY, 32, 1024), BF),
            pltpu.VMEM((CHUNKS, NY - 1, 32, 1024), BF),
            pltpu.VMEM((16, 512), F32),
            pltpu.VMEM((NZ - 1, 16, 512), BF),
            pltpu.VMEM((NZ - 1, 16, 512), BF),
            pltpu.VMEM((1024, 256), BF),
            pltpu.VMEM((1024, 256), BF),
            pltpu.VMEM((256, 1024), BF),
            dma((3,)), dma((3,)),
            dma((17,)), dma((17,)), dma, dma((16,)), dma((CHUNKS,)), dma((CHUNKS,)), dma((CHUNKS,)), dma,
            dma((17,)), dma((17,)), dma, dma((16,)), dma((CHUNKS,)), dma((CHUNKS,)), dma((CHUNKS,)), dma,
        ],
        compiler_params=pltpu.CompilerParams(
            collective_id=0, has_side_effects=True, vmem_limit_bytes=48 * 1024 * 1024
        ),
        cost_estimate=pl.CostEstimate(flops=2200000000, bytes_accessed=3200000, transcendentals=16384),
    )(activations, out_grad, w_gate, w_up, w_down)


def solution(mesh):
    in_specs = (
        P(("cols", "depth"), "rows"),
        P(("cols", "depth"), "rows"),
        P("rows", ("cols", "depth")),
        P("rows", ("cols", "depth")),
        P(("cols", "depth"), "rows"),
    )
    out_specs = (
        P(("cols", "depth"), "rows"),
        P("rows", ("cols", "depth")),
        P("rows", ("cols", "depth")),
        P(("cols", "depth"), "rows"),
    )
    return jax.shard_map(body, mesh=mesh, in_specs=in_specs, out_specs=out_specs, check_vma=False)
```

```python
import jax
import jax.numpy as jnp
from jax import lax
from jax.experimental import pallas as pl
from jax.experimental.pallas import tpu as pltpu
from jax.sharding import PartitionSpec as P

BF = jnp.bfloat16
F32 = jnp.float32
NR, NY, NZ, ZLO = 8, 4, 16, 8
CHUNKS = 4
OWN = 15
WA = 256
NT = (((1,), (1,)), ((), ()))
TN = (((0,), (0,)), ((), ()))


ORDER = (
    ("relay_b", 0), ("relay_a", 0), ("relay_b", 1), ("partial", 0), ("relay_a", 1), ("relay_b", 2), ("relay_a", 2),
    ("partial", 1), ("point", 0), ("relay_b", 3), ("partial", 2), ("point", 1), ("terms", 0), ("partial", 3),
    ("point", 2), ("terms", 1), ("reduce", 0), ("point", 3), ("terms", 2), ("reduce", 1), ("terms", 3), ("grads", 0),
    ("reduce", 2), ("reduce", 3),
)


def dot(a, b, dims=(((1,), (0,)), ((), ()))):
    return lax.dot_general(a, b, dims, preferred_element_type=F32)


def kernel(
    act_ref, grad_ref, wg_hbm, wu_hbm, wd_hbm,
    ig_hbm, gg_hbm, ug_hbm, dg_hbm,
    xa, xb, acts, grads, wg, wu, wd, part, own_part, bsend, brecv, delta,
    total, own_total, ysend, yrecv, own_z, zsend, zrecv, ig, gg, ug, dg,
    w_sem, o_sem, xa_recv, xb_recv, y0_recv, y_recv, b_recv, c_recv, dy_recv, dz_recv,
    xa_send, xb_send, y0_send, y_send, b_send, c_send, dy_send, dz_send,
):
    r = lax.axis_index("rows")
    zl = lax.axis_index("cols")
    dp = lax.axis_index("depth")
    y = lax.rem(dp, NY)
    z = lax.div(dp, NY) * ZLO + zl

    def row_peer(k):
        return {"rows": lax.rem(r + k, NR), "cols": zl, "depth": dp}

    def y_peer(k):
        return {"rows": r, "cols": zl, "depth": dp - y + lax.rem(y + k, NY)}

    def z_peer(k):
        t = lax.rem(z + (k + NZ), NZ)
        return {"rows": r, "cols": lax.rem(t, ZLO), "depth": lax.div(t, ZLO) * NY + y}

    def send(src, dst, ssem, rsem, dev):
        pltpu.make_async_remote_copy(
            src_ref=src, dst_ref=dst, send_sem=ssem, recv_sem=rsem,
            device_id=dev, device_id_type=pl.DeviceIdType.MESH,
        ).start()

    def drain(ref, sem):
        pltpu.make_async_copy(ref, ref, sem).wait()

    w_copies = [
        pltpu.make_async_copy(src, dst, w_sem.at[i])
        for i, (src, dst) in enumerate(((wg_hbm, wg), (wu_hbm, wu), (wd_hbm, wd)))
    ]
    for c in w_copies:
        c.start()

    mine = jnp.concatenate([act_ref[...].astype(F32), grad_ref[...].astype(F32)], axis=0).astype(BF)
    xa[OWN, y] = mine[:, :WA]
    xb[OWN, y] = mine[:, WA:]

    barrier = pltpu.get_barrier_semaphore()
    peers = [row_peer(k) for k in range(1, NR)]
    peers += [y_peer(k) for k in range(1, NY)]
    peers += [z_peer(k) for k in range(1, NZ)]
    for p in peers:
        pl.semaphore_signal(barrier, inc=1, device_id=p, device_id_type=pl.DeviceIdType.MESH)
    pl.semaphore_wait(barrier, len(peers))

    def y_forward(slot):
        for k in range(1, NY):
            send(xb.at[slot, y], xb.at[slot, y], y_send.at[slot], y_recv.at[slot], y_peer(k))

    def start_gather():
        for k in range(1, NY):
            send(xa.at[OWN, y], xa.at[OWN, y], y0_send, y0_recv, y_peer(k))
        for to, k in ((2, 2), (3, -2), (0, 1), (1, -1)):
            send(xb.at[OWN, y], xb.at[to, y], xb_send.at[OWN], xb_recv.at[to], z_peer(k))
        y_forward(OWN)
        drain(xa.at[OWN, pl.ds(0, 3)], y0_recv)
        for to, k in ((2, 2), (3, -2), (0, 1), (1, -1)):
            send(xa.at[OWN], xa.at[to], xa_send.at[OWN], xa_recv.at[to], z_peer(k))

    def relay_b(c):
        if c == 3:
            for slot in (12, 13, 14):
                drain(xb.at[slot, y], xb_recv.at[slot])
                y_forward(slot)
            return
        for slot in (4 * c, 4 * c + 1):
            drain(xb.at[slot, y], xb_recv.at[slot])
            y_forward(slot)
        for slot, sign in ((4 * c + 2, 1), (4 * c + 3, -1)):
            drain(xb.at[slot, y], xb_recv.at[slot])
            if c < 2:
                send(xb.at[slot, y], xb.at[slot + 4, y], xb_send.at[slot], xb_recv.at[slot + 4], z_peer(2 * sign))
            elif sign == -1:
                send(xb.at[slot, y], xb.at[14, y], xb_send.at[slot], xb_recv.at[14], z_peer(-2))
            send(xb.at[slot, y], xb.at[slot + 2, y], xb_send.at[slot], xb_recv.at[slot + 2], z_peer(sign))
            y_forward(slot)

    def relay_a(c):
        for slot, sign in ((4 * c + 2, 1), (4 * c + 3, -1)):
            drain(xa.at[slot], xa_recv.at[slot])
            if c < 2:
                send(xa.at[slot], xa.at[slot + 4], xa_send.at[slot], xa_recv.at[slot + 4], z_peer(2 * sign))
            else:
                half = pl.ds(0, 2) if sign == 1 else pl.ds(2, 2)
                extra = 16 if sign == 1 else 17
                send(xa.at[slot, half], xa.at[14, half], xa_send.at[extra], xa_recv.at[extra], z_peer(2 * sign))
            send(xa.at[slot], xa.at[slot + 2], xa_send.at[slot], xa_recv.at[slot + 2], z_peer(sign))

    def gather_wait(c):
        for s in range(4 * c, 4 * c + 4):
            drain(xb.at[s, pl.ds(0, 3)], y_recv.at[s])
        if c < 3:
            for s in (4 * c, 4 * c + 1):
                drain(xa.at[s], xa_recv.at[s])
        else:
            for s in (12, 13):
                drain(xa.at[s], xa_recv.at[s])
            drain(xa.at[14, pl.ds(0, 2)], xa_recv.at[16])
            drain(xa.at[14, pl.ds(2, 2)], xa_recv.at[17])

    def partial_sums(c):
        gather_wait(c)

        def pick(p, carry):
            s = 4 * c + lax.div(p, 2)
            y0 = lax.rem(p, 2) * 2
            rows = pl.ds(pl.multiple_of(c * 128 + p * 16, 16), 16)
            for buf, cols in ((xa, pl.ds(0, WA)), (xb, pl.ds(WA, 1024 - WA))):
                b0 = buf[s, y0].astype(F32)
                b1 = buf[s, y0 + 1].astype(F32)
                acts[rows, cols] = jnp.concatenate([b0[:8], b1[:8]], axis=0).astype(BF)
                grads[rows, cols] = jnp.concatenate([b0[8:], b1[8:]], axis=0).astype(BF)
            return carry

        lax.fori_loop(0, 8, pick, 0)
        rows = pl.ds(c * 128, 128)
        part[:, 0:256] = dot(acts[rows], wg[...])
        part[:, 256:512] = dot(acts[rows], wu[...])
        part[:, 512:768] = dot(grads[rows], wd[...], NT)
        bsend[c] = part[...].astype(BF).reshape(NR, 16, 768)
        own_part[c] = part[pl.ds(pl.multiple_of(r * 16, 16), 16)]
        for k in range(1, NR):
            send(bsend.at[c, lax.rem(r + k, NR)], brecv.at[c, k - 1], b_send.at[c], b_recv.at[c], row_peer(k))

    def pointwise(c):
        drain(brecv.at[c], b_recv.at[c])
        tot = own_part[c]
        for k in range(NR - 1):
            tot = tot + brecv[c, k].astype(F32)
        gate, up, hid = tot[:, 0:256], tot[:, 256:512], tot[:, 512:768]
        sig = 1.0 / (1.0 + jnp.exp(-gate))
        delta[c, r, :, 0:256] = (gate * sig * up).astype(BF)
        delta[c, r, :, 256:512] = (hid * up * sig * (1.0 + gate * (1.0 - sig))).astype(BF)
        delta[c, r, :, 512:768] = (hid * gate * sig).astype(BF)
        for k in range(1, NR):
            send(delta.at[c, r], delta.at[c, r], c_send.at[c], c_recv.at[c], row_peer(k))

    def input_terms(c):
        drain(delta.at[c, pl.ds(0, NR - 1)], c_recv.at[c])
        dl = delta[c].reshape(128, 768)
        total[...] = (dot(dl[:, 256:512], wg[...], NT) + dot(dl[:, 512:768], wu[...], NT)).reshape(4, NY, 8, 1024)
        for t in range(NY):
            ysend[c, t] = jnp.concatenate([total[s, t] for s in range(4)], axis=0).astype(BF)
        for s in range(4):
            own_total[c, s] = total[s, y]
        for k in range(1, NY):
            send(ysend.at[c, lax.rem(y + k, NY)], yrecv.at[c, k - 1], dy_send.at[c], dy_recv.at[c], y_peer(k))

    def slot_offset(slot):
        if slot == 14:
            return 8
        c, s = divmod(slot, 4)
        return (2 * c + 1 + s // 2) * (1 if s % 2 else -1)

    def reduce_y(c):
        drain(yrecv.at[c], dy_recv.at[c])
        for s in range(4):
            slot = 4 * c + s
            if s % 2 == 0:
                got = [yrecv[c, k, 8 * s:8 * s + 16, :].astype(F32) for k in range(NY - 1)]
            lo = 8 * (s % 2)
            v = own_total[c, s] + (got[0][lo:lo + 8] + got[1][lo:lo + 8] + got[2][lo:lo + 8])
            v = jnp.concatenate([v[:, :512], v[:, 512:]], axis=0)
            if slot == OWN:
                own_z[...] = v
            else:
                zsend[slot] = v.astype(BF)
        for s in range(4):
            slot = 4 * c + s
            if slot != OWN:
                k = slot_offset(slot) % NZ
                send(zsend.at[slot], zrecv.at[k - 1], dz_send, dz_recv, z_peer(k))

    def reduce_z():
        drain(zrecv, dz_recv)
        v = own_z[...]
        for k in range(NZ - 1):
            v = v + zrecv[k].astype(F32)
        ig[...] = jnp.concatenate([v[:8], v[8:]], axis=1).astype(BF)

    def weight_grads():
        dl = delta[...].reshape(512, 768)
        gg[...] = dot(acts[...], dl[:, 256:512], TN).astype(BF)
        ug[...] = dot(acts[...], dl[:, 512:768], TN).astype(BF)
        dg[...] = dot(dl[:, 0:256], grads[...], TN).astype(BF)

    out_copies = [
        pltpu.make_async_copy(src, dst, o_sem.at[i])
        for i, (src, dst) in enumerate(((gg, gg_hbm), (ug, ug_hbm), (dg, dg_hbm)))
    ]

    start_gather()
    for c in w_copies:
        c.wait()
    for stage, c in ORDER:
        if stage == "grads":
            weight_grads()
            for copy in out_copies:
                copy.start()
        else:
            {"relay_b": relay_b, "relay_a": relay_a, "partial": partial_sums, "point": pointwise,
             "terms": input_terms, "reduce": reduce_y}[stage](c)
    drain(xa.at[0, pl.ds(0, 3)], y0_send)
    drain(xa.at[pl.ds(0, 4)], xa_send.at[OWN])
    drain(xb.at[0], xb_send.at[OWN])
    for s in (2, 3, 6, 7):
        drain(xa.at[pl.ds(0, 2)], xa_send.at[s])
        drain(xb.at[0, pl.ds(0, 2)], xb_send.at[s])
    for s in (10, 11):
        drain(xa.at[0], xa_send.at[s])
        drain(xb.at[0, pl.ds(0, s - 9)], xb_send.at[s])
    for s in (16, 17):
        drain(xa.at[0, pl.ds(0, 2)], xa_send.at[s])
    for s in range(16):
        drain(xb.at[s, pl.ds(0, 3)], y_send.at[s])
    for c in range(CHUNKS):
        drain(brecv.at[c], b_send.at[c])
        drain(delta.at[c, pl.ds(0, NR - 1)], c_send.at[c])
        drain(yrecv.at[c], dy_send.at[c])
    for c in out_copies:
        c.wait()
    reduce_z()
    ig_copy = pltpu.make_async_copy(ig, ig_hbm, o_sem.at[3])
    ig_copy.start()
    drain(zsend, dz_send)
    ig_copy.wait()


def copy_kernel(*refs):
    n = len(refs) // 3
    ins, outs, bufs, sems = refs[:n], refs[n:2 * n], refs[2 * n:3 * n], refs[3 * n]
    loads = [pltpu.make_async_copy(ins[i], bufs[i], sems.at[0, i]) for i in range(n)]
    stores = [pltpu.make_async_copy(bufs[i], outs[i], sems.at[1, i]) for i in range(n)]
    for c in loads:
        c.start()
    for load, store in zip(loads, stores):
        load.wait()
        store.start()
    for c in stores:
        c.wait()


def write_out(*arrays):
    hbm = pl.BlockSpec(memory_space=pltpu.HBM)
    return pl.pallas_call(
        copy_kernel,
        out_shape=tuple(jax.ShapeDtypeStruct(a.shape, a.dtype) for a in arrays),
        in_specs=[pl.BlockSpec(memory_space=pl.ANY)] * len(arrays),
        out_specs=(hbm,) * len(arrays),
        scratch_shapes=[pltpu.VMEM(a.shape, a.dtype) for a in arrays]
        + [pltpu.SemaphoreType.DMA((2, len(arrays)))],
        compiler_params=pltpu.CompilerParams(vmem_limit_bytes=60 * 1024 * 1024),
    )(*arrays)


def body(activations, out_grad, w_gate, w_up, w_down):
    vmem = pl.BlockSpec(memory_space=pltpu.VMEM)
    hbm = pl.BlockSpec(memory_space=pltpu.HBM)
    any_space = pl.BlockSpec(memory_space=pl.ANY)
    dma = pltpu.SemaphoreType.DMA
    outs = pl.pallas_call(
        kernel,
        out_shape=(
            jax.ShapeDtypeStruct((8, 1024), BF),
            jax.ShapeDtypeStruct((1024, 256), BF),
            jax.ShapeDtypeStruct((1024, 256), BF),
            jax.ShapeDtypeStruct((256, 1024), BF),
        ),
        in_specs=[vmem, vmem, hbm, hbm, hbm],
        out_specs=(any_space, any_space, any_space, any_space),
        scratch_shapes=[
            pltpu.VMEM((16, 4, 16, WA), BF),
            pltpu.VMEM((16, 4, 16, 1024 - WA), BF),
            pltpu.VMEM((512, 1024), BF),
            pltpu.VMEM((512, 1024), BF),
            pltpu.VMEM((1024, 256), BF),
            pltpu.VMEM((1024, 256), BF),
            pltpu.VMEM((256, 1024), BF),
            pltpu.VMEM((128, 768), F32),
            pltpu.VMEM((CHUNKS, 16, 768), F32),
            pltpu.VMEM((CHUNKS, NR, 16, 768), BF),
            pltpu.VMEM((CHUNKS, NR - 1, 16, 768), BF),
            pltpu.VMEM((CHUNKS, NR, 16, 768), BF),
            pltpu.VMEM((4, NY, 8, 1024), F32),
            pltpu.VMEM((CHUNKS, 4, 8, 1024), F32),
            pltpu.VMEM((CHUNKS, NY, 32, 1024), BF),
            pltpu.VMEM((CHUNKS, NY - 1, 32, 1024), BF),
            pltpu.VMEM((16, 512), F32),
            pltpu.VMEM((NZ - 1, 16, 512), BF),
            pltpu.VMEM((NZ - 1, 16, 512), BF),
            pltpu.VMEM((8, 1024), BF),
            pltpu.VMEM((1024, 256), BF),
            pltpu.VMEM((1024, 256), BF),
            pltpu.VMEM((256, 1024), BF),
            dma((3,)), dma((4,)),
            dma((18,)), dma((16,)), dma, dma((16,)), dma((CHUNKS,)), dma((CHUNKS,)), dma((CHUNKS,)), dma,
            dma((18,)), dma((16,)), dma, dma((16,)), dma((CHUNKS,)), dma((CHUNKS,)), dma((CHUNKS,)), dma,
        ],
        compiler_params=pltpu.CompilerParams(
            collective_id=0, has_side_effects=True, vmem_limit_bytes=60 * 1024 * 1024
        ),
        cost_estimate=pl.CostEstimate(flops=2200000000, bytes_accessed=3200000, transcendentals=16384),
    )(activations, out_grad, w_gate, w_up, w_down)
    return write_out(*outs)


def solution(mesh):
    in_specs = (
        P(("cols", "depth"), "rows"),
        P(("cols", "depth"), "rows"),
        P("rows", ("cols", "depth")),
        P("rows", ("cols", "depth")),
        P(("cols", "depth"), "rows"),
    )
    out_specs = (
        P(("cols", "depth"), "rows"),
        P("rows", ("cols", "depth")),
        P("rows", ("cols", "depth")),
        P(("cols", "depth"), "rows"),
    )
    return jax.shard_map(body, mesh=mesh, in_specs=in_specs, out_specs=out_specs, check_vma=False)
```

```python
import jax
import jax.numpy as jnp
from jax import lax
from jax.experimental import pallas as pl
from jax.experimental.pallas import tpu as pltpu
from jax.sharding import PartitionSpec as P

BF = jnp.bfloat16
F32 = jnp.float32
NR, NY, NZ, ZLO = 8, 4, 16, 8
CHUNKS = 8
OWN = 15
WA = 256
NT = (((1,), (1,)), ((), ()))
TN = (((0,), (0,)), ((), ()))


ORDER = (
    ("relay_b", 0), ("relay_a", 0), ("relay_b", 1), ("partial", 0), ("relay_a", 1), ("partial", 1),
    ("relay_b", 2), ("relay_a", 2), ("partial", 2), ("point", 0), ("partial", 3), ("point", 1),
    ("relay_b", 3), ("partial", 4), ("point", 2), ("terms", 0), ("partial", 5), ("point", 3),
    ("terms", 1), ("partial", 6), ("point", 4), ("terms", 2), ("reduce", 0), ("partial", 7),
    ("point", 5), ("terms", 3), ("reduce", 1), ("point", 6), ("terms", 4), ("reduce", 2),
    ("point", 7), ("terms", 5), ("reduce", 3), ("terms", 6), ("reduce", 4), ("terms", 7),
    ("reduce", 5), ("grads", 0), ("reduce", 6), ("reduce", 7),
)


def dot(a, b, dims=(((1,), (0,)), ((), ()))):
    return lax.dot_general(a, b, dims, preferred_element_type=F32)


def kernel(
    act_ref, grad_ref, wg_hbm, wu_hbm, wd_hbm,
    ig_hbm, gg_hbm, ug_hbm, dg_hbm,
    xa, xb, acts, grads, wg, wu, wd, part, own_part, bsend, brecv, delta, deltas,
    total, own_total, ysend, yrecv, own_z, zsend, zrecv, ig, gg, ug, dg,
    w_sem, o_sem, xa_recv, xb_recv, y0_recv, y_recv, b_recv, c_recv, dy_recv, dz_recv,
    xa_send, xb_send, y0_send, y_send, b_send, c_send, dy_send, dz_send,
):
    r = lax.axis_index("rows")
    zl = lax.axis_index("cols")
    dp = lax.axis_index("depth")
    y = lax.rem(dp, NY)
    z = lax.div(dp, NY) * ZLO + zl

    def row_peer(k):
        return {"rows": lax.rem(r + k, NR), "cols": zl, "depth": dp}

    def y_peer(k):
        return {"rows": r, "cols": zl, "depth": dp - y + lax.rem(y + k, NY)}

    def z_peer(k):
        t = lax.rem(z + (k + NZ), NZ)
        return {"rows": r, "cols": lax.rem(t, ZLO), "depth": lax.div(t, ZLO) * NY + y}

    def send(src, dst, ssem, rsem, dev):
        pltpu.make_async_remote_copy(
            src_ref=src, dst_ref=dst, send_sem=ssem, recv_sem=rsem,
            device_id=dev, device_id_type=pl.DeviceIdType.MESH,
        ).start()

    def drain(ref, sem):
        pltpu.make_async_copy(ref, ref, sem).wait()

    w_copies = [
        pltpu.make_async_copy(src, dst, w_sem.at[i])
        for i, (src, dst) in enumerate(((wg_hbm, wg), (wu_hbm, wu), (wd_hbm, wd)))
    ]
    for c in w_copies:
        c.start()

    mine = jnp.concatenate([act_ref[...].astype(F32), grad_ref[...].astype(F32)], axis=0).astype(BF)
    xa[OWN, y] = mine[:, :WA]
    xb[OWN, y] = mine[:, WA:]

    barrier = pltpu.get_barrier_semaphore()
    peers = [row_peer(k) for k in range(1, NR)]
    peers += [y_peer(k) for k in range(1, NY)]
    peers += [z_peer(k) for k in range(1, NZ)]
    for p in peers:
        pl.semaphore_signal(barrier, inc=1, device_id=p, device_id_type=pl.DeviceIdType.MESH)
    pl.semaphore_wait(barrier, len(peers))

    def y_forward(slot):
        for k in range(1, NY):
            send(xb.at[slot, y], xb.at[slot, y], y_send.at[slot], y_recv.at[slot], y_peer(k))

    def start_gather():
        for k in range(1, NY):
            send(xa.at[OWN, y], xa.at[OWN, y], y0_send, y0_recv, y_peer(k))
        for to, k in ((2, 2), (3, -2), (0, 1), (1, -1)):
            send(xb.at[OWN, y], xb.at[to, y], xb_send.at[OWN], xb_recv.at[to], z_peer(k))
        y_forward(OWN)
        drain(xa.at[OWN, pl.ds(0, 3)], y0_recv)
        for to, k in ((2, 2), (3, -2), (0, 1), (1, -1)):
            send(xa.at[OWN], xa.at[to], xa_send.at[OWN], xa_recv.at[to], z_peer(k))

    def relay_b(c):
        if c == 3:
            for slot in (12, 13, 14):
                drain(xb.at[slot, y], xb_recv.at[slot])
                y_forward(slot)
            return
        for slot in (4 * c, 4 * c + 1):
            drain(xb.at[slot, y], xb_recv.at[slot])
            y_forward(slot)
        for slot, sign in ((4 * c + 2, 1), (4 * c + 3, -1)):
            drain(xb.at[slot, y], xb_recv.at[slot])
            if c < 2:
                send(xb.at[slot, y], xb.at[slot + 4, y], xb_send.at[slot], xb_recv.at[slot + 4], z_peer(2 * sign))
            elif sign == -1:
                send(xb.at[slot, y], xb.at[14, y], xb_send.at[slot], xb_recv.at[14], z_peer(-2))
            send(xb.at[slot, y], xb.at[slot + 2, y], xb_send.at[slot], xb_recv.at[slot + 2], z_peer(sign))
            y_forward(slot)

    def relay_a(c):
        for slot, sign in ((4 * c + 2, 1), (4 * c + 3, -1)):
            drain(xa.at[slot], xa_recv.at[slot])
            if c < 2:
                send(xa.at[slot], xa.at[slot + 4], xa_send.at[slot], xa_recv.at[slot + 4], z_peer(2 * sign))
            else:
                half = pl.ds(0, 2) if sign == 1 else pl.ds(2, 2)
                extra = 16 if sign == 1 else 17
                send(xa.at[slot, half], xa.at[14, half], xa_send.at[extra], xa_recv.at[extra], z_peer(2 * sign))
            send(xa.at[slot], xa.at[slot + 2], xa_send.at[slot], xa_recv.at[slot + 2], z_peer(sign))

    def gather_wait(c):
        for s in (2 * c, 2 * c + 1):
            drain(xb.at[s, pl.ds(0, 3)], y_recv.at[s])
            if c % 2 == 0:
                drain(xa.at[s], xa_recv.at[s])
        if c == 7:
            drain(xa.at[14, pl.ds(0, 2)], xa_recv.at[16])
            drain(xa.at[14, pl.ds(2, 2)], xa_recv.at[17])

    def partial_sums(c):
        gather_wait(c)

        def pick(p, carry):
            s = 2 * c + lax.div(p, 2)
            y0 = lax.rem(p, 2) * 2
            rows = pl.ds(pl.multiple_of(c * 64 + p * 16, 16), 16)
            for buf, cols in ((xa, pl.ds(0, WA)), (xb, pl.ds(WA, 1024 - WA))):
                b0 = buf[s, y0].astype(F32)
                b1 = buf[s, y0 + 1].astype(F32)
                acts[rows, cols] = jnp.concatenate([b0[:8], b1[:8]], axis=0).astype(BF)
                grads[rows, cols] = jnp.concatenate([b0[8:], b1[8:]], axis=0).astype(BF)
            return carry

        lax.fori_loop(0, 4, pick, 0)
        rows = pl.ds(c * 64, 64)
        part[:, 0:256] = dot(acts[rows], wg[...])
        part[:, 256:512] = dot(acts[rows], wu[...])
        part[:, 512:768] = dot(grads[rows], wd[...], NT)
        for k in range(NR):
            v = part[8 * k:8 * k + 8, :]
            bsend[c, k] = jnp.concatenate([v[:, :384], v[:, 384:]], axis=0).astype(BF)
        own_part[c] = part[pl.ds(pl.multiple_of(r * 8, 8), 8)]
        for k in range(1, NR):
            send(bsend.at[c, lax.rem(r + k, NR)], brecv.at[c, k - 1], b_send.at[c], b_recv.at[c], row_peer(k))

    def pointwise(c):
        drain(brecv.at[c], b_recv.at[c])
        tot = own_part[c]
        tot = jnp.concatenate([tot[:, :384], tot[:, 384:]], axis=0)
        for k in range(NR - 1):
            tot = tot + brecv[c, k].astype(F32)
        tot = jnp.concatenate([tot[:8], tot[8:]], axis=1)
        gate, up, hid = tot[:, 0:256], tot[:, 256:512], tot[:, 512:768]
        sig = 1.0 / (1.0 + jnp.exp(-gate))
        hidden = gate * sig * up
        gate_delta = hid * up * sig * (1.0 + gate * (1.0 - sig))
        up_delta = hid * gate * sig
        first = jnp.concatenate([hidden, gate_delta[:, :128]], axis=1)
        second = jnp.concatenate([gate_delta[:, 128:], up_delta], axis=1)
        delta[c, r] = jnp.concatenate([first, second], axis=0).astype(BF)
        for k in range(1, NR):
            send(delta.at[c, r], delta.at[c, r], c_send.at[c], c_recv.at[c], row_peer(k))

    def input_terms(c):
        drain(delta.at[c, pl.ds(0, NR - 1)], c_recv.at[c])
        for k in range(0, NR, 2):
            v0 = delta[c, k].astype(F32)
            v1 = delta[c, k + 1].astype(F32)
            rows = slice(c * 64 + 8 * k, c * 64 + 8 * k + 16)
            deltas[rows, 0:384] = jnp.concatenate([v0[:8], v1[:8]], axis=0).astype(BF)
            deltas[rows, 384:768] = jnp.concatenate([v0[8:], v1[8:]], axis=0).astype(BF)
        dl = deltas[c * 64:c * 64 + 64, :]
        total[...] = (dot(dl[:, 256:512], wg[...], NT) + dot(dl[:, 512:768], wu[...], NT)).reshape(2, NY, 8, 1024)
        for k in range(NY):
            ysend[c, k] = jnp.concatenate([total[0, k], total[1, k]], axis=0).astype(BF)
        for s in range(2):
            own_total[c, s] = total[s, y]
        for k in range(1, NY):
            send(ysend.at[c, lax.rem(y + k, NY)], yrecv.at[c, k - 1], dy_send.at[c], dy_recv.at[c], y_peer(k))

    def slot_offset(slot):
        if slot == 14:
            return 8
        return (slot // 2 + 1) * (1 if slot % 2 else -1)

    def reduce_y(c):
        drain(yrecv.at[c], dy_recv.at[c])
        got = [yrecv[c, k].astype(F32) for k in range(NY - 1)]
        for s in range(2):
            slot = 2 * c + s
            lo = 8 * s
            v = own_total[c, s] + (got[0][lo:lo + 8] + got[1][lo:lo + 8] + got[2][lo:lo + 8])
            v = jnp.concatenate([v[:, :512], v[:, 512:]], axis=0)
            if slot == OWN:
                own_z[...] = v
            else:
                zsend[slot] = v.astype(BF)
                k = slot_offset(slot) % NZ
                send(zsend.at[slot], zrecv.at[k - 1], dz_send, dz_recv, z_peer(k))

    def reduce_z():
        drain(zrecv, dz_recv)
        v = own_z[...]
        for k in range(NZ - 1):
            v = v + zrecv[k].astype(F32)
        ig[...] = jnp.concatenate([v[:8], v[8:]], axis=1).astype(BF)

    def weight_grads():
        dl = deltas[...]
        gg[...] = dot(acts[...], dl[:, 256:512], TN).astype(BF)
        ug[...] = dot(acts[...], dl[:, 512:768], TN).astype(BF)
        dg[...] = dot(dl[:, 0:256], grads[...], TN).astype(BF)

    out_copies = [
        pltpu.make_async_copy(src, dst, o_sem.at[i])
        for i, (src, dst) in enumerate(((gg, gg_hbm), (ug, ug_hbm), (dg, dg_hbm)))
    ]

    start_gather()
    for c in w_copies:
        c.wait()
    for stage, c in ORDER:
        if stage == "grads":
            weight_grads()
            for copy in out_copies:
                copy.start()
        else:
            {"relay_b": relay_b, "relay_a": relay_a, "partial": partial_sums, "point": pointwise,
             "terms": input_terms, "reduce": reduce_y}[stage](c)
    drain(xa.at[0, pl.ds(0, 3)], y0_send)
    drain(xa.at[pl.ds(0, 4)], xa_send.at[OWN])
    drain(xb.at[0], xb_send.at[OWN])
    for s in (2, 3, 6, 7):
        drain(xa.at[pl.ds(0, 2)], xa_send.at[s])
        drain(xb.at[0, pl.ds(0, 2)], xb_send.at[s])
    for s in (10, 11):
        drain(xa.at[0], xa_send.at[s])
        drain(xb.at[0, pl.ds(0, s - 9)], xb_send.at[s])
    for s in (16, 17):
        drain(xa.at[0, pl.ds(0, 2)], xa_send.at[s])
    for s in range(16):
        drain(xb.at[s, pl.ds(0, 3)], y_send.at[s])
    for c in range(CHUNKS):
        drain(brecv.at[c], b_send.at[c])
        drain(delta.at[c, pl.ds(0, NR - 1)], c_send.at[c])
        drain(yrecv.at[c], dy_send.at[c])
    for c in out_copies:
        c.wait()
    reduce_z()
    ig_copy = pltpu.make_async_copy(ig, ig_hbm, o_sem.at[3])
    ig_copy.start()
    drain(zsend, dz_send)
    ig_copy.wait()


def copy_kernel(*refs):
    n = len(refs) // 3
    ins, outs, bufs, sems = refs[:n], refs[n:2 * n], refs[2 * n:3 * n], refs[3 * n]
    loads = [pltpu.make_async_copy(ins[i], bufs[i], sems.at[0, i]) for i in range(n)]
    stores = [pltpu.make_async_copy(bufs[i], outs[i], sems.at[1, i]) for i in range(n)]
    for c in loads:
        c.start()
    for load, store in zip(loads, stores):
        load.wait()
        store.start()
    for c in stores:
        c.wait()


def write_out(*arrays):
    hbm = pl.BlockSpec(memory_space=pltpu.HBM)
    return pl.pallas_call(
        copy_kernel,
        out_shape=tuple(jax.ShapeDtypeStruct(a.shape, a.dtype) for a in arrays),
        in_specs=[pl.BlockSpec(memory_space=pl.ANY)] * len(arrays),
        out_specs=(hbm,) * len(arrays),
        scratch_shapes=[pltpu.VMEM(a.shape, a.dtype) for a in arrays]
        + [pltpu.SemaphoreType.DMA((2, len(arrays)))],
        compiler_params=pltpu.CompilerParams(vmem_limit_bytes=60 * 1024 * 1024),
    )(*arrays)


def body(activations, out_grad, w_gate, w_up, w_down):
    vmem = pl.BlockSpec(memory_space=pltpu.VMEM)
    hbm = pl.BlockSpec(memory_space=pltpu.HBM)
    any_space = pl.BlockSpec(memory_space=pl.ANY)
    dma = pltpu.SemaphoreType.DMA
    outs = pl.pallas_call(
        kernel,
        out_shape=(
            jax.ShapeDtypeStruct((8, 1024), BF),
            jax.ShapeDtypeStruct((1024, 256), BF),
            jax.ShapeDtypeStruct((1024, 256), BF),
            jax.ShapeDtypeStruct((256, 1024), BF),
        ),
        in_specs=[vmem, vmem, hbm, hbm, hbm],
        out_specs=(any_space, any_space, any_space, any_space),
        scratch_shapes=[
            pltpu.VMEM((16, 4, 16, WA), BF),
            pltpu.VMEM((16, 4, 16, 1024 - WA), BF),
            pltpu.VMEM((512, 1024), BF),
            pltpu.VMEM((512, 1024), BF),
            pltpu.VMEM((1024, 256), BF),
            pltpu.VMEM((1024, 256), BF),
            pltpu.VMEM((256, 1024), BF),
            pltpu.VMEM((64, 768), F32),
            pltpu.VMEM((CHUNKS, 8, 768), F32),
            pltpu.VMEM((CHUNKS, NR, 16, 384), BF),
            pltpu.VMEM((CHUNKS, NR - 1, 16, 384), BF),
            pltpu.VMEM((CHUNKS, NR, 16, 384), BF),
            pltpu.VMEM((512, 768), BF),
            pltpu.VMEM((2, NY, 8, 1024), F32),
            pltpu.VMEM((CHUNKS, 2, 8, 1024), F32),
            pltpu.VMEM((CHUNKS, NY, 16, 1024), BF),
            pltpu.VMEM((CHUNKS, NY - 1, 16, 1024), BF),
            pltpu.VMEM((16, 512), F32),
            pltpu.VMEM((NZ - 1, 16, 512), BF),
            pltpu.VMEM((NZ - 1, 16, 512), BF),
            pltpu.VMEM((8, 1024), BF),
            pltpu.VMEM((1024, 256), BF),
            pltpu.VMEM((1024, 256), BF),
            pltpu.VMEM((256, 1024), BF),
            dma((3,)), dma((4,)),
            dma((18,)), dma((16,)), dma, dma((16,)), dma((CHUNKS,)), dma((CHUNKS,)), dma((CHUNKS,)), dma,
            dma((18,)), dma((16,)), dma, dma((16,)), dma((CHUNKS,)), dma((CHUNKS,)), dma((CHUNKS,)), dma,
        ],
        compiler_params=pltpu.CompilerParams(
            collective_id=0, has_side_effects=True, vmem_limit_bytes=60 * 1024 * 1024
        ),
        cost_estimate=pl.CostEstimate(flops=2200000000, bytes_accessed=3200000, transcendentals=16384),
    )(activations, out_grad, w_gate, w_up, w_down)
    return write_out(*outs)


def solution(mesh):
    in_specs = (
        P(("cols", "depth"), "rows"),
        P(("cols", "depth"), "rows"),
        P("rows", ("cols", "depth")),
        P("rows", ("cols", "depth")),
        P(("cols", "depth"), "rows"),
    )
    out_specs = (
        P(("cols", "depth"), "rows"),
        P("rows", ("cols", "depth")),
        P("rows", ("cols", "depth")),
        P(("cols", "depth"), "rows"),
    )
    return jax.shard_map(body, mesh=mesh, in_specs=in_specs, out_specs=out_specs, check_vma=False)
```

```python
import jax
import jax.numpy as jnp
from jax import lax
from jax.experimental import pallas as pl
from jax.experimental.pallas import tpu as pltpu
from jax.sharding import PartitionSpec as P

BF = jnp.bfloat16
F32 = jnp.float32
NR, NY, NZ, ZLO = 8, 4, 16, 8
CHUNKS = 8
OWN = 15
WA = 256
FAR_ROWS = (4, 3, 5, 2, 6, 1, 7)
FAR_Y = (2, 1, 3)
NT = (((1,), (1,)), ((), ()))
TN = (((0,), (0,)), ((), ()))


ORDER = (
    ("relay_b", 0), ("relay_a", 0), ("relay_b", 1), ("partial", 0), ("relay_a", 1), ("partial", 1),
    ("relay_b", 2), ("relay_a", 2), ("partial", 2), ("point", 0), ("partial", 3), ("point", 1),
    ("relay_b", 3), ("partial", 4), ("point", 2), ("terms", 0), ("partial", 5), ("point", 3),
    ("terms", 1), ("partial", 6), ("point", 4), ("terms", 2), ("reduce", 0), ("partial", 7),
    ("point", 5), ("terms", 3), ("reduce", 1), ("point", 6), ("terms", 4), ("reduce", 2),
    ("point", 7), ("terms", 5), ("reduce", 3), ("terms", 6), ("reduce", 4), ("terms", 7),
    ("reduce", 5), ("grads", 0), ("reduce", 6), ("reduce", 7),
)


def dot(a, b, dims=(((1,), (0,)), ((), ()))):
    return lax.dot_general(a, b, dims, preferred_element_type=F32)


def kernel(
    act_hbm, grad_hbm, wg_hbm, wu_hbm, wd_hbm,
    ig_hbm, gg_hbm, ug_hbm, dg_hbm,
    act_ref, grad_ref, xa, xb, acts, grads, wg, wu, wd, part, own_part, bsend, brecv, delta, deltas,
    total, own_total, ysend, yrecv, own_z, zsend, zrecv, ig, gg, ug, dg,
    in_sem, w_sem, o_sem, xa_recv, xb_recv, y0_recv, y_recv, b_recv, c_recv, dy_recv, dz_recv,
    xa_send, xb_send, y0_send, y_send, b_send, c_send, dy_send, dz_send,
):
    r = lax.axis_index("rows")
    zl = lax.axis_index("cols")
    dp = lax.axis_index("depth")
    y = lax.rem(dp, NY)
    z = lax.div(dp, NY) * ZLO + zl

    def row_peer(k):
        return {"rows": lax.rem(r + k, NR), "cols": zl, "depth": dp}

    def y_peer(k):
        return {"rows": r, "cols": zl, "depth": dp - y + lax.rem(y + k, NY)}

    def z_peer(k):
        t = lax.rem(z + (k + NZ), NZ)
        return {"rows": r, "cols": lax.rem(t, ZLO), "depth": lax.div(t, ZLO) * NY + y}

    def send(src, dst, ssem, rsem, dev):
        pltpu.make_async_remote_copy(
            src_ref=src, dst_ref=dst, send_sem=ssem, recv_sem=rsem,
            device_id=dev, device_id_type=pl.DeviceIdType.MESH,
        ).start()

    def drain(ref, sem):
        pltpu.make_async_copy(ref, ref, sem).wait()

    in_copies = [
        pltpu.make_async_copy(act_hbm, act_ref, in_sem.at[0]),
        pltpu.make_async_copy(grad_hbm, grad_ref, in_sem.at[1]),
    ]
    for c in in_copies:
        c.start()

    barrier = pltpu.get_barrier_semaphore()
    peers = [row_peer(k) for k in range(1, NR)]
    peers += [y_peer(k) for k in range(1, NY)]
    peers += [z_peer(k) for k in range(1, NZ)]
    for p in peers:
        pl.semaphore_signal(barrier, inc=1, device_id=p, device_id_type=pl.DeviceIdType.MESH)

    w_copies = [
        pltpu.make_async_copy(src, dst, w_sem.at[i])
        for i, (src, dst) in enumerate(((wg_hbm, wg), (wu_hbm, wu), (wd_hbm, wd)))
    ]
    for c in w_copies:
        c.start()

    for c in in_copies:
        c.wait()

    mine = jnp.concatenate([act_ref[...].astype(F32), grad_ref[...].astype(F32)], axis=0).astype(BF)
    xa[OWN, y] = mine[:, :WA]
    xb[OWN, y] = mine[:, WA:]
    pl.semaphore_wait(barrier, len(peers))

    def y_forward(slot):
        for k in FAR_Y:
            send(xb.at[slot, y], xb.at[slot, y], y_send.at[slot], y_recv.at[slot], y_peer(k))

    def start_gather():
        for k in FAR_Y:
            send(xa.at[OWN, y], xa.at[OWN, y], y0_send, y0_recv, y_peer(k))
        for to, k in ((2, 2), (3, -2), (0, 1), (1, -1)):
            send(xb.at[OWN, y], xb.at[to, y], xb_send.at[OWN], xb_recv.at[to], z_peer(k))
        y_forward(OWN)
        drain(xa.at[OWN, pl.ds(0, 3)], y0_recv)
        for to, k in ((2, 2), (3, -2), (0, 1), (1, -1)):
            send(xa.at[OWN], xa.at[to], xa_send.at[OWN], xa_recv.at[to], z_peer(k))

    def relay_b(c):
        if c == 3:
            for slot in (12, 13, 14):
                drain(xb.at[slot, y], xb_recv.at[slot])
                y_forward(slot)
            return
        for slot in (4 * c, 4 * c + 1):
            drain(xb.at[slot, y], xb_recv.at[slot])
            y_forward(slot)
        for slot, sign in ((4 * c + 2, 1), (4 * c + 3, -1)):
            drain(xb.at[slot, y], xb_recv.at[slot])
            if c < 2:
                send(xb.at[slot, y], xb.at[slot + 4, y], xb_send.at[slot], xb_recv.at[slot + 4], z_peer(2 * sign))
            elif sign == -1:
                send(xb.at[slot, y], xb.at[14, y], xb_send.at[slot], xb_recv.at[14], z_peer(-2))
            send(xb.at[slot, y], xb.at[slot + 2, y], xb_send.at[slot], xb_recv.at[slot + 2], z_peer(sign))
            y_forward(slot)

    def relay_a(c):
        for slot, sign in ((4 * c + 2, 1), (4 * c + 3, -1)):
            drain(xa.at[slot], xa_recv.at[slot])
            if c < 2:
                send(xa.at[slot], xa.at[slot + 4], xa_send.at[slot], xa_recv.at[slot + 4], z_peer(2 * sign))
            else:
                half = pl.ds(0, 2) if sign == 1 else pl.ds(2, 2)
                extra = 16 if sign == 1 else 17
                send(xa.at[slot, half], xa.at[14, half], xa_send.at[extra], xa_recv.at[extra], z_peer(2 * sign))
            send(xa.at[slot], xa.at[slot + 2], xa_send.at[slot], xa_recv.at[slot + 2], z_peer(sign))

    def gather_wait(c):
        for s in (2 * c, 2 * c + 1):
            drain(xb.at[s, pl.ds(0, 3)], y_recv.at[s])
            if c % 2 == 0:
                drain(xa.at[s], xa_recv.at[s])
        if c == 7:
            drain(xa.at[14, pl.ds(0, 2)], xa_recv.at[16])
            drain(xa.at[14, pl.ds(2, 2)], xa_recv.at[17])

    def partial_sums(c):
        gather_wait(c)

        def pick(p, carry):
            s = 2 * c + lax.div(p, 2)
            y0 = lax.rem(p, 2) * 2
            rows = pl.ds(pl.multiple_of(c * 64 + p * 16, 16), 16)
            for buf, cols in ((xa, pl.ds(0, WA)), (xb, pl.ds(WA, 1024 - WA))):
                b0 = buf[s, y0].astype(F32)
                b1 = buf[s, y0 + 1].astype(F32)
                acts[rows, cols] = jnp.concatenate([b0[:8], b1[:8]], axis=0).astype(BF)
                grads[rows, cols] = jnp.concatenate([b0[8:], b1[8:]], axis=0).astype(BF)
            return carry

        lax.fori_loop(0, 4, pick, 0)
        rows = pl.ds(c * 64, 64)
        part[:, 0:256] = dot(acts[rows], wg[...])
        part[:, 256:512] = dot(acts[rows], wu[...])
        part[:, 512:768] = dot(grads[rows], wd[...], NT)
        for k in range(NR):
            v = part[8 * k:8 * k + 8, :]
            bsend[c, k] = jnp.concatenate([v[:, :384], v[:, 384:]], axis=0).astype(BF)
        own_part[c] = part[pl.ds(pl.multiple_of(r * 8, 8), 8)]
        for k in FAR_ROWS:
            send(bsend.at[c, lax.rem(r + k, NR)], brecv.at[c, k - 1], b_send.at[c], b_recv.at[c], row_peer(k))

    def pointwise(c):
        drain(brecv.at[c], b_recv.at[c])
        tot = own_part[c]
        tot = jnp.concatenate([tot[:, :384], tot[:, 384:]], axis=0)
        for k in range(NR - 1):
            tot = tot + brecv[c, k].astype(F32)
        tot = jnp.concatenate([tot[:8], tot[8:]], axis=1)
        gate, up, hid = tot[:, 0:256], tot[:, 256:512], tot[:, 512:768]
        sig = 1.0 / (1.0 + jnp.exp(-gate))
        hidden = gate * sig * up
        gate_delta = hid * up * sig * (1.0 + gate * (1.0 - sig))
        up_delta = hid * gate * sig
        first = jnp.concatenate([hidden, gate_delta[:, :128]], axis=1)
        second = jnp.concatenate([gate_delta[:, 128:], up_delta], axis=1)
        delta[c, r] = jnp.concatenate([first, second], axis=0).astype(BF)
        for k in FAR_ROWS:
            send(delta.at[c, r], delta.at[c, r], c_send.at[c], c_recv.at[c], row_peer(k))

    def input_terms(c):
        drain(delta.at[c, pl.ds(0, NR - 1)], c_recv.at[c])
        for k in range(0, NR, 2):
            v0 = delta[c, k].astype(F32)
            v1 = delta[c, k + 1].astype(F32)
            rows = slice(c * 64 + 8 * k, c * 64 + 8 * k + 16)
            deltas[rows, 0:384] = jnp.concatenate([v0[:8], v1[:8]], axis=0).astype(BF)
            deltas[rows, 384:768] = jnp.concatenate([v0[8:], v1[8:]], axis=0).astype(BF)
        dl = deltas[c * 64:c * 64 + 64, :]
        total[...] = (dot(dl[:, 256:512], wg[...], NT) + dot(dl[:, 512:768], wu[...], NT)).reshape(2, NY, 8, 1024)
        for k in range(NY):
            ysend[c, k] = jnp.concatenate([total[0, k], total[1, k]], axis=0).astype(BF)
        for s in range(2):
            own_total[c, s] = total[s, y]
        for k in FAR_Y:
            send(ysend.at[c, lax.rem(y + k, NY)], yrecv.at[c, k - 1], dy_send.at[c], dy_recv.at[c], y_peer(k))

    def slot_offset(slot):
        if slot == 14:
            return 8
        return (slot // 2 + 1) * (1 if slot % 2 else -1)

    def reduce_y(c):
        drain(yrecv.at[c], dy_recv.at[c])
        got = [yrecv[c, k].astype(F32) for k in range(NY - 1)]
        for s in range(2):
            slot = 2 * c + s
            lo = 8 * s
            v = own_total[c, s] + (got[0][lo:lo + 8] + got[1][lo:lo + 8] + got[2][lo:lo + 8])
            v = jnp.concatenate([v[:, :512], v[:, 512:]], axis=0)
            if slot == OWN:
                own_z[...] = v
            else:
                zsend[slot] = v.astype(BF)
                k = slot_offset(slot) % NZ
                send(zsend.at[slot], zrecv.at[k - 1], dz_send, dz_recv, z_peer(k))

    def reduce_z():
        drain(zrecv, dz_recv)
        v = own_z[...]
        for k in range(NZ - 1):
            v = v + zrecv[k].astype(F32)
        ig[...] = jnp.concatenate([v[:8], v[8:]], axis=1).astype(BF)

    def weight_grads():
        dl = deltas[...]
        gg[...] = dot(acts[...], dl[:, 256:512], TN).astype(BF)
        ug[...] = dot(acts[...], dl[:, 512:768], TN).astype(BF)
        dg[...] = dot(dl[:, 0:256], grads[...], TN).astype(BF)

    out_copies = [
        pltpu.make_async_copy(src, dst, o_sem.at[i])
        for i, (src, dst) in enumerate(((gg, gg_hbm), (ug, ug_hbm), (dg, dg_hbm)))
    ]

    start_gather()
    for c in w_copies:
        c.wait()
    for stage, c in ORDER:
        if stage == "grads":
            weight_grads()
            for copy in out_copies:
                copy.start()
        else:
            {"relay_b": relay_b, "relay_a": relay_a, "partial": partial_sums, "point": pointwise,
             "terms": input_terms, "reduce": reduce_y}[stage](c)
    drain(xa.at[0, pl.ds(0, 3)], y0_send)
    drain(xa.at[pl.ds(0, 4)], xa_send.at[OWN])
    drain(xb.at[0], xb_send.at[OWN])
    for s in (2, 3, 6, 7):
        drain(xa.at[pl.ds(0, 2)], xa_send.at[s])
        drain(xb.at[0, pl.ds(0, 2)], xb_send.at[s])
    for s in (10, 11):
        drain(xa.at[0], xa_send.at[s])
        drain(xb.at[0, pl.ds(0, s - 9)], xb_send.at[s])
    for s in (16, 17):
        drain(xa.at[0, pl.ds(0, 2)], xa_send.at[s])
    for s in range(16):
        drain(xb.at[s, pl.ds(0, 3)], y_send.at[s])
    for c in range(CHUNKS):
        drain(brecv.at[c], b_send.at[c])
        drain(delta.at[c, pl.ds(0, NR - 1)], c_send.at[c])
        drain(yrecv.at[c], dy_send.at[c])
    for c in out_copies:
        c.wait()
    reduce_z()
    ig_copy = pltpu.make_async_copy(ig, ig_hbm, o_sem.at[3])
    ig_copy.start()
    drain(zsend, dz_send)
    ig_copy.wait()


def copy_kernel(*refs):
    n = len(refs) // 3
    ins, outs, bufs, sems = refs[:n], refs[n:2 * n], refs[2 * n:3 * n], refs[3 * n]
    loads = [pltpu.make_async_copy(ins[i], bufs[i], sems.at[0, i]) for i in range(n)]
    stores = [pltpu.make_async_copy(bufs[i], outs[i], sems.at[1, i]) for i in range(n)]
    for c in loads:
        c.start()
    for load, store in zip(loads, stores):
        load.wait()
        store.start()
    for c in stores:
        c.wait()


def write_out(*arrays):
    hbm = pl.BlockSpec(memory_space=pltpu.HBM)
    return pl.pallas_call(
        copy_kernel,
        out_shape=tuple(jax.ShapeDtypeStruct(a.shape, a.dtype) for a in arrays),
        in_specs=[pl.BlockSpec(memory_space=pl.ANY)] * len(arrays),
        out_specs=(hbm,) * len(arrays),
        scratch_shapes=[pltpu.VMEM(a.shape, a.dtype) for a in arrays]
        + [pltpu.SemaphoreType.DMA((2, len(arrays)))],
        compiler_params=pltpu.CompilerParams(vmem_limit_bytes=60 * 1024 * 1024),
    )(*arrays)


def body(activations, out_grad, w_gate, w_up, w_down):
    hbm = pl.BlockSpec(memory_space=pltpu.HBM)
    any_space = pl.BlockSpec(memory_space=pl.ANY)
    dma = pltpu.SemaphoreType.DMA
    outs = pl.pallas_call(
        kernel,
        out_shape=(
            jax.ShapeDtypeStruct((8, 1024), BF),
            jax.ShapeDtypeStruct((1024, 256), BF),
            jax.ShapeDtypeStruct((1024, 256), BF),
            jax.ShapeDtypeStruct((256, 1024), BF),
        ),
        in_specs=[hbm] * 5,
        out_specs=(any_space, any_space, any_space, any_space),
        scratch_shapes=[
            pltpu.VMEM((8, 1024), BF),
            pltpu.VMEM((8, 1024), BF),
            pltpu.VMEM((16, 4, 16, WA), BF),
            pltpu.VMEM((16, 4, 16, 1024 - WA), BF),
            pltpu.VMEM((512, 1024), BF),
            pltpu.VMEM((512, 1024), BF),
            pltpu.VMEM((1024, 256), BF),
            pltpu.VMEM((1024, 256), BF),
            pltpu.VMEM((256, 1024), BF),
            pltpu.VMEM((64, 768), F32),
            pltpu.VMEM((CHUNKS, 8, 768), F32),
            pltpu.VMEM((CHUNKS, NR, 16, 384), BF),
            pltpu.VMEM((CHUNKS, NR - 1, 16, 384), BF),
            pltpu.VMEM((CHUNKS, NR, 16, 384), BF),
            pltpu.VMEM((512, 768), BF),
            pltpu.VMEM((2, NY, 8, 1024), F32),
            pltpu.VMEM((CHUNKS, 2, 8, 1024), F32),
            pltpu.VMEM((CHUNKS, NY, 16, 1024), BF),
            pltpu.VMEM((CHUNKS, NY - 1, 16, 1024), BF),
            pltpu.VMEM((16, 512), F32),
            pltpu.VMEM((NZ - 1, 16, 512), BF),
            pltpu.VMEM((NZ - 1, 16, 512), BF),
            pltpu.VMEM((8, 1024), BF),
            pltpu.VMEM((1024, 256), BF),
            pltpu.VMEM((1024, 256), BF),
            pltpu.VMEM((256, 1024), BF),
            dma((2,)), dma((3,)), dma((4,)),
            dma((18,)), dma((16,)), dma, dma((16,)), dma((CHUNKS,)), dma((CHUNKS,)), dma((CHUNKS,)), dma,
            dma((18,)), dma((16,)), dma, dma((16,)), dma((CHUNKS,)), dma((CHUNKS,)), dma((CHUNKS,)), dma,
        ],
        compiler_params=pltpu.CompilerParams(
            collective_id=0, has_side_effects=True, vmem_limit_bytes=60 * 1024 * 1024
        ),
        cost_estimate=pl.CostEstimate(flops=2200000000, bytes_accessed=3200000, transcendentals=16384),
    )(activations, out_grad, w_gate, w_up, w_down)
    return write_out(*outs)


def solution(mesh):
    in_specs = (
        P(("cols", "depth"), "rows"),
        P(("cols", "depth"), "rows"),
        P("rows", ("cols", "depth")),
        P("rows", ("cols", "depth")),
        P(("cols", "depth"), "rows"),
    )
    out_specs = (
        P(("cols", "depth"), "rows"),
        P("rows", ("cols", "depth")),
        P("rows", ("cols", "depth")),
        P(("cols", "depth"), "rows"),
    )
    return jax.shard_map(body, mesh=mesh, in_specs=in_specs, out_specs=out_specs, check_vma=False)
```

```python
import jax
import jax.numpy as jnp
from jax import lax
from jax.experimental import pallas as pl
from jax.experimental.pallas import tpu as pltpu
from jax.sharding import PartitionSpec as P

BF = jnp.bfloat16
F32 = jnp.float32
NR, NY, NZ, ZLO = 8, 4, 16, 8
CHUNKS = 8
OWN = 15
WA = 256
FAR_ROWS = (4, 3, 5, 2, 6, 1, 7)
FAR_Y = (2, 1, 3)
NT = (((1,), (1,)), ((), ()))
TN = (((0,), (0,)), ((), ()))


ORDER = (
    ("relay_b", 0), ("relay_a", 0), ("relay_b", 1), ("partial", 0), ("relay_a", 1), ("partial", 1),
    ("relay_b", 2), ("relay_a", 2), ("partial", 2), ("point", 0), ("partial", 3), ("point", 1),
    ("relay_b", 3), ("partial", 4), ("point", 2), ("terms", 0), ("partial", 5), ("point", 3),
    ("terms", 1), ("partial", 6), ("point", 4), ("terms", 2), ("reduce", 0), ("partial", 7),
    ("point", 5), ("terms", 3), ("reduce", 1), ("point", 6), ("terms", 4), ("reduce", 2),
    ("point", 7), ("terms", 5), ("reduce", 3), ("terms", 6), ("reduce", 4), ("terms", 7),
    ("reduce", 5), ("grads", 0), ("reduce", 6), ("reduce", 7),
)


def dot(a, b, dims=(((1,), (0,)), ((), ()))):
    return lax.dot_general(a, b, dims, preferred_element_type=F32)


def kernel(
    act_hbm, grad_hbm, wg_hbm, wu_hbm, wd_hbm,
    ig_hbm, gg_hbm, ug_hbm, dg_hbm,
    act_ref, grad_ref, xa, xb, acts, grads, wg, wu, wd, part, own_part, bsend, brecv, delta, deltas,
    total, own_total, ysend, yrecv, own_z, zsend, zrecv, ig, gg, ug, dg,
    in_sem, w_sem, o_sem, xa_recv, xb_recv, y0_recv, y_recv, b_recv, c_recv, dy_recv, dz_recv,
    xa_send, xb_send, y0_send, y_send, b_send, c_send, dy_send, dz_send,
):
    r = lax.axis_index("rows")
    zl = lax.axis_index("cols")
    dp = lax.axis_index("depth")
    y = lax.rem(dp, NY)
    z = lax.div(dp, NY) * ZLO + zl

    def row_peer(k):
        return {"rows": lax.rem(r + k, NR), "cols": zl, "depth": dp}

    def y_peer(k):
        return {"rows": r, "cols": zl, "depth": dp - y + lax.rem(y + k, NY)}

    def z_peer(k):
        t = lax.rem(z + (k + NZ), NZ)
        return {"rows": r, "cols": lax.rem(t, ZLO), "depth": lax.div(t, ZLO) * NY + y}

    def send(src, dst, ssem, rsem, dev):
        pltpu.make_async_remote_copy(
            src_ref=src, dst_ref=dst, send_sem=ssem, recv_sem=rsem,
            device_id=dev, device_id_type=pl.DeviceIdType.MESH,
        ).start()

    def drain(ref, sem):
        pltpu.make_async_copy(ref, ref, sem).wait()

    in_copies = [
        pltpu.make_async_copy(act_hbm, act_ref, in_sem.at[0]),
        pltpu.make_async_copy(grad_hbm, grad_ref, in_sem.at[1]),
    ]
    for c in in_copies:
        c.start()

    barrier = pltpu.get_barrier_semaphore()
    peers = [z_peer(k) for k in (8, 7, 9, 6, 10, 5, 11, 4, 12, 3, 13, 2, 14)]
    peers += [row_peer(k) for k in FAR_ROWS]
    peers += [y_peer(k) for k in FAR_Y]
    peers += [z_peer(k) for k in (1, 15)]
    for p in peers:
        pl.semaphore_signal(barrier, inc=1, device_id=p, device_id_type=pl.DeviceIdType.MESH)

    w_copies = [
        pltpu.make_async_copy(src, dst, w_sem.at[i])
        for i, (src, dst) in enumerate(((wg_hbm, wg), (wu_hbm, wu), (wd_hbm, wd)))
    ]
    for c in w_copies:
        c.start()

    for c in in_copies:
        c.wait()

    mine = jnp.concatenate([act_ref[...].astype(F32), grad_ref[...].astype(F32)], axis=0).astype(BF)
    xa[OWN, y] = mine[:, :WA]
    xb[OWN, y] = mine[:, WA:]
    pl.semaphore_wait(barrier, len(peers))

    def y_forward(slot):
        for k in FAR_Y:
            send(xb.at[slot, y], xb.at[slot, y], y_send.at[slot], y_recv.at[slot], y_peer(k))

    def start_gather():
        for k in FAR_Y:
            send(xa.at[OWN, y], xa.at[OWN, y], y0_send, y0_recv, y_peer(k))
        for to, k in ((2, 2), (3, -2), (0, 1), (1, -1)):
            send(xb.at[OWN, y], xb.at[to, y], xb_send.at[OWN], xb_recv.at[to], z_peer(k))
        y_forward(OWN)
        drain(xa.at[OWN, pl.ds(0, 3)], y0_recv)
        for to, k in ((2, 2), (3, -2), (0, 1), (1, -1)):
            send(xa.at[OWN], xa.at[to], xa_send.at[OWN], xa_recv.at[to], z_peer(k))

    def relay_b(c):
        if c == 3:
            for slot in (12, 13, 14):
                drain(xb.at[slot, y], xb_recv.at[slot])
                y_forward(slot)
            return
        for slot in (4 * c, 4 * c + 1):
            drain(xb.at[slot, y], xb_recv.at[slot])
            y_forward(slot)
        for slot, sign in ((4 * c + 2, 1), (4 * c + 3, -1)):
            drain(xb.at[slot, y], xb_recv.at[slot])
            if c < 2:
                send(xb.at[slot, y], xb.at[slot + 4, y], xb_send.at[slot], xb_recv.at[slot + 4], z_peer(2 * sign))
            elif sign == -1:
                send(xb.at[slot, y], xb.at[14, y], xb_send.at[slot], xb_recv.at[14], z_peer(-2))
            send(xb.at[slot, y], xb.at[slot + 2, y], xb_send.at[slot], xb_recv.at[slot + 2], z_peer(sign))
            y_forward(slot)

    def relay_a(c):
        for slot, sign in ((4 * c + 2, 1), (4 * c + 3, -1)):
            drain(xa.at[slot], xa_recv.at[slot])
            if c < 2:
                send(xa.at[slot], xa.at[slot + 4], xa_send.at[slot], xa_recv.at[slot + 4], z_peer(2 * sign))
            else:
                half = pl.ds(0, 2) if sign == 1 else pl.ds(2, 2)
                extra = 16 if sign == 1 else 17
                send(xa.at[slot, half], xa.at[14, half], xa_send.at[extra], xa_recv.at[extra], z_peer(2 * sign))
            send(xa.at[slot], xa.at[slot + 2], xa_send.at[slot], xa_recv.at[slot + 2], z_peer(sign))

    def gather_wait(c):
        for s in (2 * c, 2 * c + 1):
            drain(xb.at[s, pl.ds(0, 3)], y_recv.at[s])
            if c % 2 == 0:
                drain(xa.at[s], xa_recv.at[s])
        if c == 7:
            drain(xa.at[14, pl.ds(0, 2)], xa_recv.at[16])
            drain(xa.at[14, pl.ds(2, 2)], xa_recv.at[17])

    def partial_sums(c):
        gather_wait(c)

        def pick(p, carry):
            s = 2 * c + lax.div(p, 2)
            y0 = lax.rem(p, 2) * 2
            rows = pl.ds(pl.multiple_of(c * 64 + p * 16, 16), 16)
            for buf, cols in ((xa, pl.ds(0, WA)), (xb, pl.ds(WA, 1024 - WA))):
                b0 = buf[s, y0].astype(F32)
                b1 = buf[s, y0 + 1].astype(F32)
                acts[rows, cols] = jnp.concatenate([b0[:8], b1[:8]], axis=0).astype(BF)
                grads[rows, cols] = jnp.concatenate([b0[8:], b1[8:]], axis=0).astype(BF)
            return carry

        lax.fori_loop(0, 4, pick, 0)
        rows = pl.ds(c * 64, 64)
        part[:, 0:256] = dot(acts[rows], wg[...])
        part[:, 256:512] = dot(acts[rows], wu[...])
        part[:, 512:768] = dot(grads[rows], wd[...], NT)
        for k in range(NR):
            v = part[8 * k:8 * k + 8, :]
            bsend[c, k] = jnp.concatenate([v[:, :384], v[:, 384:]], axis=0).astype(BF)
        own_part[c] = part[pl.ds(pl.multiple_of(r * 8, 8), 8)]
        for k in FAR_ROWS:
            send(bsend.at[c, lax.rem(r + k, NR)], brecv.at[c, k - 1], b_send.at[c], b_recv.at[c], row_peer(k))

    def pointwise(c):
        drain(brecv.at[c], b_recv.at[c])
        tot = own_part[c]
        tot = jnp.concatenate([tot[:, :384], tot[:, 384:]], axis=0)
        for k in range(NR - 1):
            tot = tot + brecv[c, k].astype(F32)
        tot = jnp.concatenate([tot[:8], tot[8:]], axis=1)
        gate, up, hid = tot[:, 0:256], tot[:, 256:512], tot[:, 512:768]
        sig = 1.0 / (1.0 + jnp.exp(-gate))
        hidden = gate * sig * up
        gate_delta = hid * up * sig * (1.0 + gate * (1.0 - sig))
        up_delta = hid * gate * sig
        first = jnp.concatenate([hidden, gate_delta[:, :128]], axis=1)
        second = jnp.concatenate([gate_delta[:, 128:], up_delta], axis=1)
        delta[c, r] = jnp.concatenate([first, second], axis=0).astype(BF)
        for k in FAR_ROWS:
            send(delta.at[c, r], delta.at[c, r], c_send.at[c], c_recv.at[c], row_peer(k))

    def input_terms(c):
        drain(delta.at[c, pl.ds(0, NR - 1)], c_recv.at[c])
        for k in range(0, NR, 2):
            v0 = delta[c, k].astype(F32)
            v1 = delta[c, k + 1].astype(F32)
            rows = slice(c * 64 + 8 * k, c * 64 + 8 * k + 16)
            deltas[rows, 0:384] = jnp.concatenate([v0[:8], v1[:8]], axis=0).astype(BF)
            deltas[rows, 384:768] = jnp.concatenate([v0[8:], v1[8:]], axis=0).astype(BF)
        dl = deltas[c * 64:c * 64 + 64, :]
        total[...] = (dot(dl[:, 256:512], wg[...], NT) + dot(dl[:, 512:768], wu[...], NT)).reshape(2, NY, 8, 1024)
        for k in range(NY):
            ysend[c, k] = jnp.concatenate([total[0, k], total[1, k]], axis=0).astype(BF)
        for s in range(2):
            own_total[c, s] = total[s, y]
        for k in FAR_Y:
            send(ysend.at[c, lax.rem(y + k, NY)], yrecv.at[c, k - 1], dy_send.at[c], dy_recv.at[c], y_peer(k))

    def slot_offset(slot):
        if slot == 14:
            return 8
        return (slot // 2 + 1) * (1 if slot % 2 else -1)

    def reduce_y(c):
        drain(yrecv.at[c], dy_recv.at[c])
        got = [yrecv[c, k].astype(F32) for k in range(NY - 1)]
        for s in range(2):
            slot = 2 * c + s
            lo = 8 * s
            v = own_total[c, s] + (got[0][lo:lo + 8] + got[1][lo:lo + 8] + got[2][lo:lo + 8])
            v = jnp.concatenate([v[:, :512], v[:, 512:]], axis=0)
            if slot == OWN:
                own_z[...] = v
            else:
                zsend[slot] = v.astype(BF)
                k = slot_offset(slot) % NZ
                send(zsend.at[slot], zrecv.at[k - 1], dz_send, dz_recv, z_peer(k))

    def reduce_z():
        drain(zrecv, dz_recv)
        v = own_z[...]
        for k in range(NZ - 1):
            v = v + zrecv[k].astype(F32)
        ig[...] = jnp.concatenate([v[:8], v[8:]], axis=1).astype(BF)

    def weight_grads():
        dl = deltas[...]
        gg[...] = dot(acts[...], dl[:, 256:512], TN).astype(BF)
        ug[...] = dot(acts[...], dl[:, 512:768], TN).astype(BF)
        dg[...] = dot(dl[:, 0:256], grads[...], TN).astype(BF)

    out_copies = [
        pltpu.make_async_copy(src, dst, o_sem.at[i])
        for i, (src, dst) in enumerate(((gg, gg_hbm), (ug, ug_hbm), (dg, dg_hbm)))
    ]

    start_gather()
    for c in w_copies:
        c.wait()
    for stage, c in ORDER:
        if stage == "grads":
            weight_grads()
            for copy in out_copies:
                copy.start()
        else:
            {"relay_b": relay_b, "relay_a": relay_a, "partial": partial_sums, "point": pointwise,
             "terms": input_terms, "reduce": reduce_y}[stage](c)
    drain(xa.at[0, pl.ds(0, 3)], y0_send)
    drain(xa.at[pl.ds(0, 4)], xa_send.at[OWN])
    drain(xb.at[0], xb_send.at[OWN])
    for s in (2, 3, 6, 7):
        drain(xa.at[pl.ds(0, 2)], xa_send.at[s])
        drain(xb.at[0, pl.ds(0, 2)], xb_send.at[s])
    for s in (10, 11):
        drain(xa.at[0], xa_send.at[s])
        drain(xb.at[0, pl.ds(0, s - 9)], xb_send.at[s])
    for s in (16, 17):
        drain(xa.at[0, pl.ds(0, 2)], xa_send.at[s])
    for s in range(16):
        drain(xb.at[s, pl.ds(0, 3)], y_send.at[s])
    for c in range(CHUNKS):
        drain(brecv.at[c], b_send.at[c])
        drain(delta.at[c, pl.ds(0, NR - 1)], c_send.at[c])
        drain(yrecv.at[c], dy_send.at[c])
    for c in out_copies:
        c.wait()
    reduce_z()
    ig_copy = pltpu.make_async_copy(ig, ig_hbm, o_sem.at[3])
    ig_copy.start()
    drain(zsend, dz_send)
    ig_copy.wait()


def copy_kernel(*refs):
    n = len(refs) // 3
    ins, outs, bufs, sems = refs[:n], refs[n:2 * n], refs[2 * n:3 * n], refs[3 * n]
    loads = [pltpu.make_async_copy(ins[i], bufs[i], sems.at[0, i]) for i in range(n)]
    stores = [pltpu.make_async_copy(bufs[i], outs[i], sems.at[1, i]) for i in range(n)]
    for c in loads:
        c.start()
    for load, store in zip(loads, stores):
        load.wait()
        store.start()
    for c in stores:
        c.wait()


def write_out(*arrays):
    hbm = pl.BlockSpec(memory_space=pltpu.HBM)
    return pl.pallas_call(
        copy_kernel,
        out_shape=tuple(jax.ShapeDtypeStruct(a.shape, a.dtype) for a in arrays),
        in_specs=[pl.BlockSpec(memory_space=pl.ANY)] * len(arrays),
        out_specs=(hbm,) * len(arrays),
        scratch_shapes=[pltpu.VMEM(a.shape, a.dtype) for a in arrays]
        + [pltpu.SemaphoreType.DMA((2, len(arrays)))],
        compiler_params=pltpu.CompilerParams(vmem_limit_bytes=60 * 1024 * 1024),
    )(*arrays)


def body(activations, out_grad, w_gate, w_up, w_down):
    hbm = pl.BlockSpec(memory_space=pltpu.HBM)
    any_space = pl.BlockSpec(memory_space=pl.ANY)
    dma = pltpu.SemaphoreType.DMA
    outs = pl.pallas_call(
        kernel,
        out_shape=(
            jax.ShapeDtypeStruct((8, 1024), BF),
            jax.ShapeDtypeStruct((1024, 256), BF),
            jax.ShapeDtypeStruct((1024, 256), BF),
            jax.ShapeDtypeStruct((256, 1024), BF),
        ),
        in_specs=[hbm] * 5,
        out_specs=(any_space, any_space, any_space, any_space),
        scratch_shapes=[
            pltpu.VMEM((8, 1024), BF),
            pltpu.VMEM((8, 1024), BF),
            pltpu.VMEM((16, 4, 16, WA), BF),
            pltpu.VMEM((16, 4, 16, 1024 - WA), BF),
            pltpu.VMEM((512, 1024), BF),
            pltpu.VMEM((512, 1024), BF),
            pltpu.VMEM((1024, 256), BF),
            pltpu.VMEM((1024, 256), BF),
            pltpu.VMEM((256, 1024), BF),
            pltpu.VMEM((64, 768), F32),
            pltpu.VMEM((CHUNKS, 8, 768), F32),
            pltpu.VMEM((CHUNKS, NR, 16, 384), BF),
            pltpu.VMEM((CHUNKS, NR - 1, 16, 384), BF),
            pltpu.VMEM((CHUNKS, NR, 16, 384), BF),
            pltpu.VMEM((512, 768), BF),
            pltpu.VMEM((2, NY, 8, 1024), F32),
            pltpu.VMEM((CHUNKS, 2, 8, 1024), F32),
            pltpu.VMEM((CHUNKS, NY, 16, 1024), BF),
            pltpu.VMEM((CHUNKS, NY - 1, 16, 1024), BF),
            pltpu.VMEM((16, 512), F32),
            pltpu.VMEM((NZ - 1, 16, 512), BF),
            pltpu.VMEM((NZ - 1, 16, 512), BF),
            pltpu.VMEM((8, 1024), BF),
            pltpu.VMEM((1024, 256), BF),
            pltpu.VMEM((1024, 256), BF),
            pltpu.VMEM((256, 1024), BF),
            dma((2,)), dma((3,)), dma((4,)),
            dma((18,)), dma((16,)), dma, dma((16,)), dma((CHUNKS,)), dma((CHUNKS,)), dma((CHUNKS,)), dma,
            dma((18,)), dma((16,)), dma, dma((16,)), dma((CHUNKS,)), dma((CHUNKS,)), dma((CHUNKS,)), dma,
        ],
        compiler_params=pltpu.CompilerParams(
            collective_id=0, has_side_effects=True, vmem_limit_bytes=60 * 1024 * 1024
        ),
        cost_estimate=pl.CostEstimate(flops=2200000000, bytes_accessed=3200000, transcendentals=16384),
    )(activations, out_grad, w_gate, w_up, w_down)
    return write_out(*outs)


def solution(mesh):
    in_specs = (
        P(("cols", "depth"), "rows"),
        P(("cols", "depth"), "rows"),
        P("rows", ("cols", "depth")),
        P("rows", ("cols", "depth")),
        P(("cols", "depth"), "rows"),
    )
    out_specs = (
        P(("cols", "depth"), "rows"),
        P("rows", ("cols", "depth")),
        P("rows", ("cols", "depth")),
        P(("cols", "depth"), "rows"),
    )
    return jax.shard_map(body, mesh=mesh, in_specs=in_specs, out_specs=out_specs, check_vma=False)
```
